32 devices in a mesh: cb: 4 (over x, core), frame: 8 (over z, y).
Axes of the slice: x: 2, y: 2, z: 4, core: 2. Of those that a mesh axis runs over, the one named last changes fastest.
Arguments:
- inputs: bfloat16 [2048, 16, 1024], P('frame', 'cb'), may hold values from -64 to 64
- norm_gain: float32 [1024], replicated, may hold values from 0.1 to 1.9
- w_qkv: bfloat16 [16, 1024, 3072], P('cb', 'frame'), may hold values from -4 to 4
- w_out: bfloat16 [16, 1024, 1024], P('cb', 'frame'), may hold values from -0.1875 to 0.1875
- grad_out: bfloat16 [2048, 16, 1024], P('frame', 'cb'), may hold values from -6 to 6
Outputs:
- outputs: bfloat16 [2048, 16, 1024], P('frame', 'cb')
- grad_in: bfloat16 [2048, 16, 1024], P('frame', 'cb')
The draws below stay inside these ranges and needn't reach their ends.
All inputs are finite; a program needn't handle non-finite values.
Results may differ from the reference program's by a relative error of at most 0.0053.
Values may be sent and summed in bfloat16 or wider, within the bound.
No kernel may reach another device: no remote copies, remote signals or barrier semaphores. Data moves between devices by JAX's collectives and lax.ppermute only.
A program may use at most 128 MiB of HBM per device.

```python
import math
import jax
import jax.numpy as jnp
from jax import lax

D = 1024
HEADS = 16
CODEBOOKS = 16
FR_DEV = 256
FRAMES = 2048


def draw_inputs(key, part):
    key_noise, key_rows, key_cols = jax.random.split(key, 3)
    shape_full = (FRAMES, CODEBOOKS, D)
    noise = jax.random.truncated_normal(key_noise, -4.0, 4.0, shape_full, jnp.float32)
    low = math.log(0.4)
    high = math.log(4.0)
    row_scale = jnp.exp(jax.random.uniform(key_rows, (FRAMES, CODEBOOKS, 1), jnp.float32, low, high))
    col_scale = jnp.exp(jax.random.uniform(key_cols, (1, 1, D), jnp.float32, low, high))
    return (noise * row_scale * col_scale).astype(jnp.bfloat16)


def draw_w_qkv(key, part):
    key_base = jax.random.fold_in(jax.random.fold_in(key, 7), 0)
    base = jax.random.truncated_normal(key_base, -4.0, 4.0, (CODEBOOKS, D, 3 * D), jnp.float32) / math.sqrt(D)
    return base.astype(jnp.bfloat16)


def block_scale(rng, extent, cuts, smallest, top_value):
    loudness = 1.0
    for dim, blocks in cuts:
        draws = jax.random.uniform(jax.random.fold_in(jax.random.fold_in(rng, 6), dim), (blocks,), jnp.float32, smallest / len(cuts), top_value / len(cuts))
        loudness = loudness * jnp.repeat(jnp.exp(draws), extent[dim] // blocks).reshape((-1,) + (1,) * (len(extent) - 1 - dim))
    return loudness


def gaussian(key, extent, scale, limit, cuts=(), dtype=jnp.bfloat16):
    entries = scale * jax.random.normal(key, extent, jnp.float32)
    if cuts:
        entries = entries * block_scale(key, extent, cuts, -0.22, 0.18)
    return jnp.clip(entries, -limit, limit).astype(dtype)


def setup_inputs(seed: int = 0) -> dict:
    arg_keys = jax.random.split(jax.random.key(seed), 6)
    return {
        "inputs": draw_inputs(jax.random.fold_in(arg_keys[5], 71), 0),
        "norm_gain": jnp.clip(1.0 + 0.18 * jax.random.normal(arg_keys[1], (D,), jnp.float32), 0.1, 1.9),
        "w_qkv": draw_w_qkv(jax.random.fold_in(arg_keys[5], 71), 0),
        "w_out": gaussian(arg_keys[3], (CODEBOOKS, D, D), D ** -0.5, 0.1875, ((0, 4), (1, 8))),
        "grad_out": gaussian(arg_keys[4], (FRAMES, CODEBOOKS, D), 1.0, 6.0, ((0, 8), (1, 4))),
    }


epsilon = 1e-05
highest = lax.Precision.HIGHEST

def rounded(values):
    return lax.optimization_barrier(values.astype(jnp.bfloat16))

def per_codebook(operand, weight):
    return jnp.einsum('fcd,cde->fce', operand.astype(jnp.float32), weight, precision=highest)

def per_codebook_back(operand, weight):
    return jnp.einsum('fce,cde->fcd', operand.astype(jnp.float32), weight, precision=highest)

def to_heads(values, head_count):
    frames, depth, columns = values.shape
    return values.reshape(frames, depth, head_count, columns // head_count).astype(jnp.float32)

def attention_probs(queries, key_rows, head_count):
    depth = queries.shape[1]
    factor = (queries.shape[2] // head_count) ** (-0.5)
    scores = jnp.einsum('fihe,fjhe->fhij', to_heads(queries, head_count), to_heads(key_rows, head_count), precision=highest) * factor
    causal = lax.broadcasted_iota(jnp.int32, (depth, depth), 0) >= lax.broadcasted_iota(jnp.int32, (depth, depth), 1)
    scores = jnp.where(causal, scores, -jnp.inf)
    weights = jnp.exp(scores - lax.optimization_barrier(jnp.max(scores, axis=-1, keepdims=True)))
    return weights / lax.optimization_barrier(jnp.sum(weights, axis=-1, keepdims=True))

def attention_grads(queries, key_rows, values, grad_context, head_count):
    shape_full = queries.shape
    factor = (queries.shape[2] // head_count) ** (-0.5)
    probs = attention_probs(queries, key_rows, head_count)
    probs_low = rounded(probs).astype(jnp.float32)
    grad_heads = to_heads(grad_context, head_count)
    grad_values = jnp.einsum('fhij,fihe->fjhe', probs_low, grad_heads, precision=highest)
    grad_probs = jnp.einsum('fihe,fjhe->fhij', grad_heads, to_heads(values, head_count), precision=highest)
    inner = lax.optimization_barrier(jnp.sum(probs * grad_probs, axis=-1, keepdims=True))
    grad_scores = rounded(probs * (grad_probs - inner) * factor).astype(jnp.float32)
    grad_queries = jnp.einsum('fhij,fjhe->fihe', grad_scores, to_heads(key_rows, head_count), precision=highest)
    grad_keys = jnp.einsum('fhij,fihe->fjhe', grad_scores, to_heads(queries, head_count), precision=highest)
    return (rounded(grad_queries.reshape(shape_full)), rounded(grad_keys.reshape(shape_full)), rounded(grad_values.reshape(shape_full)))

def block_pass(pieces, norm_gain, w_qkv, w_out):
    inputs, grad_out = pieces
    columns = inputs.shape[2]
    wide_in = inputs.astype(jnp.float32)
    inverse_rms = lax.rsqrt(lax.optimization_barrier(jnp.mean(wide_in * wide_in, axis=-1, keepdims=True)) + epsilon)
    normed = rounded(wide_in * inverse_rms * norm_gain)
    projected = rounded(per_codebook(normed, w_qkv))
    queries = projected[:, :, :columns]
    key_rows = projected[:, :, columns:2 * columns]
    values = projected[:, :, 2 * columns:]
    probs = attention_probs(queries, key_rows, HEADS)
    probs_low = rounded(probs).astype(jnp.float32)
    mixed = jnp.einsum('fhij,fjhe->fihe', probs_low, to_heads(values, HEADS), precision=highest)
    context = rounded(mixed.reshape(inputs.shape))
    outputs = (wide_in + per_codebook(context, w_out)).astype(jnp.bfloat16)
    grad_context = rounded(per_codebook_back(grad_out, w_out))
    grad_queries, grad_keys, grad_values = attention_grads(queries, key_rows, values, grad_context, HEADS)
    grad_qkv = jnp.concatenate([grad_queries, grad_keys, grad_values], axis=-1)
    scaled = per_codebook_back(grad_qkv, w_qkv) * norm_gain
    inner = lax.optimization_barrier(jnp.mean(scaled * wide_in, axis=-1, keepdims=True))
    grad_in = grad_out.astype(jnp.float32) + inverse_rms * (scaled - wide_in * inverse_rms * inverse_rms * inner)
    return (outputs, grad_in.astype(jnp.bfloat16))

def reference(inputs, norm_gain, w_qkv, w_out, grad_out):
    blocks = FRAMES // FR_DEV
    shape_blocks = (blocks, FR_DEV) + inputs.shape[1:]
    wide_qkv = w_qkv.astype(jnp.float32)
    wide_out = w_out.astype(jnp.float32)
    outputs, grad_in = lax.map(lambda pieces: block_pass(pieces, norm_gain, wide_qkv, wide_out), (inputs.reshape(shape_blocks), grad_out.reshape(shape_blocks)))
    return (outputs.reshape(inputs.shape), grad_in.reshape(inputs.shape))
```

```python
import functools

import jax
import jax.numpy as jnp
from jax import lax
from jax.experimental import pallas as pl
from jax.experimental.pallas import tpu as pltpu
from jax.sharding import PartitionSpec as P

HEADS = 16
GROUPS = 4
EPSILON = 1e-05
F32 = jnp.float32
BF16 = jnp.bfloat16
FRAME_BLOCK = 16
HALF = 8


def params(mib):
    return pltpu.CompilerParams(
        dimension_semantics=("arbitrary",), vmem_limit_bytes=mib * 1024 * 1024
    )


def cost(flops, byte_count):
    return pl.CostEstimate(flops=flops, bytes_accessed=byte_count, transcendentals=0)


def fill(source_ref, slot_refs, whole_ref):
    depth = slot_refs[0].shape[1]
    for slot, ref in enumerate(slot_refs):
        start = pl.multiple_of(source_ref[slot] * depth, depth)
        whole_ref[pl.ds(start, depth), :] = ref[0]


def project_kernel(back, source_ref, rows_ref, *refs):
    slot_refs, out_ref, whole_ref = refs[:-2], refs[-2], refs[-1]
    fill(source_ref, slot_refs, whole_ref)
    contract = ((1,), (1,)) if back else ((1,), (0,))
    result = lax.dot_general(
        rows_ref[0], whole_ref[...], (contract, ((), ())), preferred_element_type=F32
    )
    out_ref[...] = result.astype(BF16).reshape(out_ref.shape)


def project(source, rows, slots, parts, back):
    codebooks, frames, columns = rows.shape
    depth, width = slots[0].shape[1:]
    wide = depth * len(slots)
    out_columns = wide if back else width
    share = frames // parts
    return pl.pallas_call(
        functools.partial(project_kernel, back),
        grid=(codebooks,),
        in_specs=[
            pl.BlockSpec(memory_space=pltpu.SMEM),
            pl.BlockSpec((1, frames, columns), lambda c: (c, 0, 0)),
        ]
        + [pl.BlockSpec((1, depth, width), lambda c: (c, 0, 0)) for _ in slots],
        out_specs=pl.BlockSpec((parts, 1, share, out_columns), lambda c: (0, c, 0, 0)),
        out_shape=jax.ShapeDtypeStruct((parts, codebooks, share, out_columns), BF16),
        scratch_shapes=[pltpu.VMEM((wide, width), BF16)],
        compiler_params=params(32),
        cost_estimate=cost(
            2 * codebooks * frames * wide * width, 2 * codebooks * wide * (width + 1024)
        ),
        name="project_back" if back else "project",
    )(source, rows, *slots)


def attend_kernel(heads, qkv_ref, grad_ref, out_ref):
    codebooks, _, width = grad_ref.shape
    head_width = width // heads
    rows = codebooks * HALF
    factor = head_width ** (-0.5)
    row = lax.broadcasted_iota(jnp.int32, (rows, rows), 0)
    column = lax.broadcasted_iota(jnp.int32, (rows, rows), 1)
    allowed = jnp.logical_and(row % HALF == column % HALF, row >= column)[None]
    lane_head = lax.broadcasted_iota(jnp.int32, (rows, width), 1) // head_width

    def wide(ref, first):
        values = ref[:, :, first : first + width].astype(F32)
        return values.reshape(codebooks, FRAME_BLOCK // HALF, HALF, width)

    def stacked(values):
        pieces = [jnp.where(lane_head == h, values, 0.0).astype(BF16) for h in range(heads)]
        return jnp.concatenate(pieces, axis=0)

    def beside(values):
        return jnp.concatenate([values[h * rows : (h + 1) * rows] for h in range(heads)], axis=1)

    def dot(left, right, left_dim, right_dim):
        return lax.dot_general(
            left, right, (((left_dim,), (right_dim,)), ((), ())), preferred_element_type=F32
        )

    parts = [wide(qkv_ref, 0), wide(qkv_ref, width), wide(qkv_ref, 2 * width), wide(grad_ref, 0)]
    results = [[], [], [], []]
    for half in range(FRAME_BLOCK // HALF):
        q, k, v, g = [part[:, half].reshape(rows, width) for part in parts]
        q_heads, k_heads, v_heads, g_heads = stacked(q), stacked(k), stacked(v), stacked(g)
        scores = dot(q_heads, k.astype(BF16), 1, 1).reshape(heads, rows, rows) * factor
        scores = jnp.where(allowed, scores, -jnp.inf)
        weights = jnp.exp(scores - jnp.max(scores, axis=-1, keepdims=True))
        probs = weights / jnp.sum(weights, axis=-1, keepdims=True)
        grad_probs = dot(g_heads, v.astype(BF16), 1, 1).reshape(heads, rows, rows)
        inner = jnp.sum(probs * grad_probs, axis=-1, keepdims=True)
        grad_scores = (probs * (grad_probs - inner) * factor).astype(BF16)
        probs_low = probs.astype(BF16).reshape(heads * rows, rows)
        grad_scores = grad_scores.reshape(heads * rows, rows)
        results[0].append(dot(beside(probs_low), v_heads, 1, 0))
        results[1].append(dot(beside(grad_scores), k_heads, 1, 0))
        results[2].append(dot(grad_scores, q_heads, 0, 0))
        results[3].append(dot(probs_low, g_heads, 0, 0))
    for index, halves in enumerate(results):
        halves = [value.reshape(codebooks, 1, HALF, width) for value in halves]
        whole = jnp.concatenate(halves, axis=1).reshape(codebooks, FRAME_BLOCK, width)
        out_ref[:, :, index * width : (index + 1) * width] = whole.astype(BF16)


def attend(group, heads, qkv, grad_context):
    codebooks, frames, columns = qkv.shape
    width = columns // 3
    rows = codebooks * HALF
    return pl.pallas_call(
        functools.partial(attend_kernel, heads),
        grid=(frames // FRAME_BLOCK,),
        in_specs=[
            pl.BlockSpec((codebooks, FRAME_BLOCK, columns), lambda f: (0, f, 0)),
            pl.BlockSpec((codebooks, FRAME_BLOCK, width), lambda f: (0, f, group)),
        ],
        out_specs=pl.BlockSpec((codebooks, FRAME_BLOCK, 4 * width), lambda f: (0, f, 0)),
        out_shape=jax.ShapeDtypeStruct((codebooks, frames, 4 * width), BF16),
        compiler_params=params(32),
        cost_estimate=cost(
            12 * heads * rows * rows * width * (frames // HALF),
            2 * codebooks * frames * width * 8,
        ),
        name="attend",
    )(qkv, grad_context)


def backward_kernel(first, last, source_ref, back_ref, *refs):
    refs = list(refs)
    whole_ref = refs.pop()
    out_ref = refs.pop()
    total_ref = None if first else refs.pop(0)
    if last:
        rows_ref, grad_ref, gain_ref = refs.pop(0), refs.pop(0), refs.pop(0)
    fill(source_ref, refs, whole_ref)
    frames = out_ref.shape[1]
    width = whole_ref.shape[1] // 3
    grad = back_ref[...].reshape(frames, 4 * width)[:, width:]
    total = lax.dot_general(
        grad, whole_ref[...], (((1,), (1,)), ((), ())), preferred_element_type=F32
    )
    if not first:
        total = total + total_ref[0]
    if last:
        rows = rows_ref[0].astype(F32)
        inverse_rms = lax.rsqrt(jnp.mean(rows * rows, axis=-1, keepdims=True) + EPSILON)
        scaled = total * gain_ref[...]
        inner = jnp.mean(scaled * rows, axis=-1, keepdims=True)
        total = grad_ref[0].astype(F32) + inverse_rms * (
            scaled - rows * (inverse_rms * inverse_rms * inner)
        )
    out_ref[0] = total.astype(out_ref.dtype)


def backward(source, returned, slots, total, epilogue):
    parts, codebooks, share, columns = returned.shape
    frames = parts * share
    depth, width = slots[0].shape[1:]
    wide = depth * len(slots)
    row_spec = pl.BlockSpec((1, frames, wide), lambda c: (c, 0, 0))
    operands = [source, returned]
    specs = [
        pl.BlockSpec(memory_space=pltpu.SMEM),
        pl.BlockSpec((parts, 1, share, columns), lambda c: (0, c, 0, 0)),
    ]
    if total is not None:
        operands.append(total)
        specs.append(row_spec)
    if epilogue is not None:
        rows, grad_out, gain = epilogue
        operands += [rows, grad_out, gain.reshape(1, wide)]
        specs += [row_spec, row_spec, pl.BlockSpec((1, wide), lambda c: (0, 0))]
    operands += slots
    specs += [pl.BlockSpec((1, depth, width), lambda c: (c, 0, 0)) for _ in slots]
    return pl.pallas_call(
        functools.partial(backward_kernel, total is None, epilogue is not None),
        grid=(codebooks,),
        in_specs=specs,
        out_specs=row_spec,
        out_shape=jax.ShapeDtypeStruct(
            (codebooks, frames, wide), F32 if epilogue is None else BF16
        ),
        scratch_shapes=[pltpu.VMEM((wide, width), BF16)],
        compiler_params=params(40),
        cost_estimate=cost(
            2 * codebooks * frames * wide * width, 2 * codebooks * wide * (width + 5 * frames)
        ),
        name="backward",
    )(*operands)


def output_kernel(groups, source_ref, rows_ref, *refs):
    refs = list(refs)
    whole_ref = refs.pop()
    out_ref = refs.pop()
    fill(source_ref, refs[groups:], whole_ref)
    frames = out_ref.shape[1]
    pieces = [ref[...].reshape(frames, ref.shape[3]) for ref in refs[:groups]]
    result = jnp.dot(
        jnp.concatenate(pieces, axis=1), whole_ref[...], preferred_element_type=F32
    )
    out_ref[0] = (rows_ref[0].astype(F32) + result).astype(BF16)


def output(source, rows, returned, slots):
    codebooks, frames, columns = rows.shape
    parts, _, share, group_columns = returned[0].shape
    depth, width = slots[0].shape[1:]
    row_spec = pl.BlockSpec((1, frames, columns), lambda c: (c, 0, 0))
    return pl.pallas_call(
        functools.partial(output_kernel, len(returned)),
        grid=(codebooks,),
        in_specs=[pl.BlockSpec(memory_space=pltpu.SMEM), row_spec]
        + [
            pl.BlockSpec((parts, 1, share, group_columns // 4), lambda c: (0, c, 0, 0))
            for _ in returned
        ]
        + [pl.BlockSpec((1, depth, width), lambda c: (c, 0, 0)) for _ in slots],
        out_specs=row_spec,
        out_shape=jax.ShapeDtypeStruct(rows.shape, BF16),
        scratch_shapes=[pltpu.VMEM((columns, width), BF16)],
        compiler_params=params(32),
        cost_estimate=cost(
            2 * codebooks * frames * columns * width, 2 * codebooks * columns * (width + 3 * frames)
        ),
        name="output",
    )(source, rows, *returned, *slots)


def tie(values, *after):
    return lax.optimization_barrier((values,) + after)[0]


def body(lines, columns_wide, inputs, norm_gain, w_qkv, w_out, grad_out):
    frames, codebooks, columns = inputs.shape
    parts = lax.axis_size("cb")
    place = lax.axis_index("frame")
    line_place, column_place = place // columns_wide, place % columns_wide
    count = lines * columns_wide

    right = [(i, i + columns_wide) for i in range(count - columns_wide)]
    left = [(j, i) for i, j in right]

    def turn(step):
        return [
            (i, i // columns_wide * columns_wide + (i + step) % columns_wide) for i in range(count)
        ]

    def along_line(own):
        to_right, to_left = [own], [own]
        for _ in range(lines - 1):
            to_right.append(lax.ppermute(to_right[-1], "frame", right))
            to_left.append(lax.ppermute(to_left[-1], "frame", left))
        return [own] + [
            jnp.where(line_place >= k, to_right[k], to_left[lines - k]) for k in range(1, lines)
        ]

    def across(own):
        return [own] + [lax.ppermute(own, "frame", turn(step)) for step in range(1, columns_wide)]

    order = [
        (line_place - k) % lines * columns_wide + (column_place - m) % columns_wide
        for k in range(lines)
        for m in range(columns_wide)
    ]
    source = jnp.stack(order).astype(jnp.int32)

    width = columns // GROUPS
    shards = [w_out] + [
        jnp.concatenate(
            [
                w_qkv[:, :, kind * columns + g * width : kind * columns + (g + 1) * width]
                for kind in range(3)
            ],
            axis=-1,
        )
        for g in range(GROUPS)
    ]
    lined, slots = [], []
    for index, own in enumerate(shards):
        if index >= 2:
            own = tie(own, *lined[index - 2])
        if index < len(shards) - 1:
            line = along_line(own)
            lined.append(line)
            slots.append([piece for shard in line for piece in across(shard)])
        else:
            crossed = [along_line(piece) for piece in across(own)]
            slots.append([crossed[m][k] for k in range(lines) for m in range(columns_wide)])

    wide_in = inputs.astype(F32)
    inverse_rms = lax.rsqrt(jnp.mean(wide_in * wide_in, axis=-1, keepdims=True) + EPSILON)
    normed = (wide_in * inverse_rms * norm_gain).astype(BF16).transpose(1, 0, 2)
    rows = inputs.transpose(1, 0, 2)
    grad_rows = grad_out.transpose(1, 0, 2)

    def exchange(values):
        return lax.all_to_all(values, "cb", split_axis=0, concat_axis=0, tiled=True)

    def joined(values):
        return values.reshape((values.shape[0] * values.shape[1],) + values.shape[2:])

    grad_context = joined(exchange(project(source, grad_rows, slots[0], parts, True)))
    returned, total = [], None
    for g in range(GROUPS):
        weight = slots[1 + g]
        qkv = joined(exchange(project(source, normed, weight, parts, False)))
        mixed = attend(g, HEADS // GROUPS, qkv, grad_context)
        back = exchange(mixed.reshape((parts, codebooks) + mixed.shape[1:]))
        returned.append(back)
        epilogue = (rows, grad_rows, norm_gain) if g == GROUPS - 1 else None
        total = backward(source, back, weight, total, epilogue)
    outputs = output(source, rows, returned, slots[0])
    return outputs.transpose(1, 0, 2), total.transpose(1, 0, 2)


def solution(mesh):
    count = mesh.shape["frame"]
    columns_wide = 2 if count % 2 == 0 else 1
    return jax.shard_map(
        functools.partial(body, count // columns_wide, columns_wide),
        mesh=mesh,
        in_specs=(
            P("frame", "cb", None),
            P(),
            P("cb", "frame", None),
            P("cb", "frame", None),
            P("frame", "cb", None),
        ),
        out_specs=(P("frame", "cb", None), P("frame", "cb", None)),
        check_vma=False,
    )
```

```python
import functools

import jax
import jax.numpy as jnp
from jax import lax
from jax.experimental import pallas as pl
from jax.experimental.pallas import tpu as pltpu
from jax.sharding import PartitionSpec as P

HEADS = 16
GROUPS = 4
EPSILON = 1e-05
F32 = jnp.float32
BF16 = jnp.bfloat16
FRAME_BLOCK = 16
HALF = 8


def params(mib):
    return pltpu.CompilerParams(
        dimension_semantics=("arbitrary",), vmem_limit_bytes=mib * 1024 * 1024
    )


def cost(flops, byte_count):
    return pl.CostEstimate(flops=flops, bytes_accessed=byte_count, transcendentals=0)


def fill(source_ref, slot_refs, whole_ref):
    depth = slot_refs[0].shape[1]
    for slot, ref in enumerate(slot_refs):
        start = pl.multiple_of(source_ref[slot] * depth, depth)
        whole_ref[pl.ds(start, depth), :] = ref[0]


def project_kernel(back, source_ref, rows_ref, *refs):
    slot_refs, out_ref, whole_ref = refs[:-2], refs[-2], refs[-1]
    fill(source_ref, slot_refs, whole_ref)
    contract = ((1,), (1,)) if back else ((1,), (0,))
    result = lax.dot_general(
        rows_ref[0], whole_ref[...], (contract, ((), ())), preferred_element_type=F32
    )
    out_ref[...] = result.astype(BF16).reshape(out_ref.shape)


def project(source, rows, slots, parts, back):
    codebooks, frames, columns = rows.shape
    depth, width = slots[0].shape[1:]
    wide = depth * len(slots)
    out_columns = wide if back else width
    share = frames // parts
    return pl.pallas_call(
        functools.partial(project_kernel, back),
        grid=(codebooks,),
        in_specs=[
            pl.BlockSpec(memory_space=pltpu.SMEM),
            pl.BlockSpec((1, frames, columns), lambda c: (c, 0, 0)),
        ]
        + [pl.BlockSpec((1, depth, width), lambda c: (c, 0, 0)) for _ in slots],
        out_specs=pl.BlockSpec((parts, 1, share, out_columns), lambda c: (0, c, 0, 0)),
        out_shape=jax.ShapeDtypeStruct((parts, codebooks, share, out_columns), BF16),
        scratch_shapes=[pltpu.VMEM((wide, width), BF16)],
        compiler_params=params(32),
        cost_estimate=cost(
            2 * codebooks * frames * wide * width, 2 * codebooks * wide * (width + 1024)
        ),
        name="project_back" if back else "project",
    )(source, rows, *slots)


def attend_kernel(heads, qkv_ref, grad_ref, out_ref):
    codebooks, _, width = grad_ref.shape
    head_width = width // heads
    rows = codebooks * HALF
    factor = head_width ** (-0.5)
    row = lax.broadcasted_iota(jnp.int32, (rows, rows), 0)
    column = lax.broadcasted_iota(jnp.int32, (rows, rows), 1)
    allowed = jnp.logical_and(row % HALF == column % HALF, row >= column)[None]
    lane_head = lax.broadcasted_iota(jnp.int32, (rows, width), 1) // head_width

    def wide(ref, first):
        values = ref[:, :, first : first + width].astype(F32)
        return values.reshape(codebooks, FRAME_BLOCK // HALF, HALF, width)

    def stacked(values):
        pieces = [jnp.where(lane_head == h, values, 0.0).astype(BF16) for h in range(heads)]
        return jnp.concatenate(pieces, axis=0)

    def beside(values):
        return jnp.concatenate([values[h * rows : (h + 1) * rows] for h in range(heads)], axis=1)

    def dot(left, right, left_dim, right_dim):
        return lax.dot_general(
            left, right, (((left_dim,), (right_dim,)), ((), ())), preferred_element_type=F32
        )

    parts = [wide(qkv_ref, 0), wide(qkv_ref, width), wide(qkv_ref, 2 * width), wide(grad_ref, 0)]
    results = [[], [], [], []]
    for half in range(FRAME_BLOCK // HALF):
        q, k, v, g = [part[:, half].reshape(rows, width) for part in parts]
        q_heads, k_heads, v_heads, g_heads = stacked(q), stacked(k), stacked(v), stacked(g)
        scores = dot(q_heads, k.astype(BF16), 1, 1).reshape(heads, rows, rows) * factor
        scores = jnp.where(allowed, scores, -jnp.inf)
        weights = jnp.exp(scores - jnp.max(scores, axis=-1, keepdims=True))
        probs = weights / jnp.sum(weights, axis=-1, keepdims=True)
        grad_probs = dot(g_heads, v.astype(BF16), 1, 1).reshape(heads, rows, rows)
        inner = jnp.sum(probs * grad_probs, axis=-1, keepdims=True)
        grad_scores = (probs * (grad_probs - inner) * factor).astype(BF16)
        probs_low = probs.astype(BF16).reshape(heads * rows, rows)
        grad_scores = grad_scores.reshape(heads * rows, rows)
        results[0].append(dot(beside(probs_low), v_heads, 1, 0))
        results[1].append(dot(beside(grad_scores), k_heads, 1, 0))
        results[2].append(dot(grad_scores, q_heads, 0, 0))
        results[3].append(dot(probs_low, g_heads, 0, 0))
    for index, halves in enumerate(results):
        halves = [value.reshape(codebooks, 1, HALF, width) for value in halves]
        whole = jnp.concatenate(halves, axis=1).reshape(codebooks, FRAME_BLOCK, width)
        out_ref[:, :, index * width : (index + 1) * width] = whole.astype(BF16)


def attend(group, heads, qkv, grad_context):
    codebooks, frames, columns = qkv.shape
    width = columns // 3
    rows = codebooks * HALF
    return pl.pallas_call(
        functools.partial(attend_kernel, heads),
        grid=(frames // FRAME_BLOCK,),
        in_specs=[
            pl.BlockSpec((codebooks, FRAME_BLOCK, columns), lambda f: (0, f, 0)),
            pl.BlockSpec((codebooks, FRAME_BLOCK, width), lambda f: (0, f, group)),
        ],
        out_specs=pl.BlockSpec((codebooks, FRAME_BLOCK, 4 * width), lambda f: (0, f, 0)),
        out_shape=jax.ShapeDtypeStruct((codebooks, frames, 4 * width), BF16),
        compiler_params=params(32),
        cost_estimate=cost(
            12 * heads * rows * rows * width * (frames // HALF),
            2 * codebooks * frames * width * 8,
        ),
        name="attend",
    )(qkv, grad_context)


def backward_kernel(first, last, source_ref, back_ref, *refs):
    refs = list(refs)
    whole_ref = refs.pop()
    out_ref = refs.pop()
    total_ref = None if first else refs.pop(0)
    if last:
        rows_ref, grad_ref, gain_ref = refs.pop(0), refs.pop(0), refs.pop(0)
    fill(source_ref, refs, whole_ref)
    frames = out_ref.shape[1]
    width = whole_ref.shape[1] // 3
    grad = back_ref[...].reshape(frames, 4 * width)[:, width:]
    total = lax.dot_general(
        grad, whole_ref[...], (((1,), (1,)), ((), ())), preferred_element_type=F32
    )
    if not first:
        total = total + total_ref[0]
    if last:
        rows = rows_ref[0].astype(F32)
        inverse_rms = lax.rsqrt(jnp.mean(rows * rows, axis=-1, keepdims=True) + EPSILON)
        scaled = total * gain_ref[...]
        inner = jnp.mean(scaled * rows, axis=-1, keepdims=True)
        total = grad_ref[0].astype(F32) + inverse_rms * (
            scaled - rows * (inverse_rms * inverse_rms * inner)
        )
    out_ref[0] = total.astype(out_ref.dtype)


def backward(source, returned, slots, total, epilogue):
    parts, codebooks, share, columns = returned.shape
    frames = parts * share
    depth, width = slots[0].shape[1:]
    wide = depth * len(slots)
    row_spec = pl.BlockSpec((1, frames, wide), lambda c: (c, 0, 0))
    operands = [source, returned]
    specs = [
        pl.BlockSpec(memory_space=pltpu.SMEM),
        pl.BlockSpec((parts, 1, share, columns), lambda c: (0, c, 0, 0)),
    ]
    if total is not None:
        operands.append(total)
        specs.append(row_spec)
    if epilogue is not None:
        rows, grad_out, gain = epilogue
        operands += [rows, grad_out, gain.reshape(1, wide)]
        specs += [row_spec, row_spec, pl.BlockSpec((1, wide), lambda c: (0, 0))]
    operands += slots
    specs += [pl.BlockSpec((1, depth, width), lambda c: (c, 0, 0)) for _ in slots]
    return pl.pallas_call(
        functools.partial(backward_kernel, total is None, epilogue is not None),
        grid=(codebooks,),
        in_specs=specs,
        out_specs=row_spec,
        out_shape=jax.ShapeDtypeStruct(
            (codebooks, frames, wide), F32 if epilogue is None else BF16
        ),
        scratch_shapes=[pltpu.VMEM((wide, width), BF16)],
        compiler_params=params(40),
        cost_estimate=cost(
            2 * codebooks * frames * wide * width, 2 * codebooks * wide * (width + 5 * frames)
        ),
        name="backward",
    )(*operands)


def output_kernel(groups, source_ref, rows_ref, *refs):
    refs = list(refs)
    whole_ref = refs.pop()
    out_ref = refs.pop()
    fill(source_ref, refs[groups:], whole_ref)
    frames = out_ref.shape[1]
    pieces = [ref[...].reshape(frames, ref.shape[3]) for ref in refs[:groups]]
    result = jnp.dot(
        jnp.concatenate(pieces, axis=1), whole_ref[...], preferred_element_type=F32
    )
    out_ref[0] = (rows_ref[0].astype(F32) + result).astype(BF16)


def output(source, rows, returned, slots):
    codebooks, frames, columns = rows.shape
    parts, _, share, group_columns = returned[0].shape
    depth, width = slots[0].shape[1:]
    row_spec = pl.BlockSpec((1, frames, columns), lambda c: (c, 0, 0))
    return pl.pallas_call(
        functools.partial(output_kernel, len(returned)),
        grid=(codebooks,),
        in_specs=[pl.BlockSpec(memory_space=pltpu.SMEM), row_spec]
        + [
            pl.BlockSpec((parts, 1, share, group_columns // 4), lambda c: (0, c, 0, 0))
            for _ in returned
        ]
        + [pl.BlockSpec((1, depth, width), lambda c: (c, 0, 0)) for _ in slots],
        out_specs=row_spec,
        out_shape=jax.ShapeDtypeStruct(rows.shape, BF16),
        scratch_shapes=[pltpu.VMEM((columns, width), BF16)],
        compiler_params=params(32),
        cost_estimate=cost(
            2 * codebooks * frames * columns * width, 2 * codebooks * columns * (width + 3 * frames)
        ),
        name="output",
    )(source, rows, *returned, *slots)


def tie(values, after):
    return lax.optimization_barrier((values,) + tuple(after))[0]


def body(lines, columns_wide, inputs, norm_gain, w_qkv, w_out, grad_out):
    frames, codebooks, columns = inputs.shape
    parts = lax.axis_size("cb")
    place = lax.axis_index("frame")
    line_place, column_place = place // columns_wide, place % columns_wide
    count = lines * columns_wide

    along = [(i, (i + columns_wide) % count) for i in range(count)]

    def turn(step):
        return [
            (i, i // columns_wide * columns_wide + (i + step) % columns_wide) for i in range(count)
        ]

    order = [
        (line_place - k) % lines * columns_wide + (column_place - m) % columns_wide
        for k in range(lines)
        for m in range(columns_wide)
    ]
    source = jnp.stack(order).astype(jnp.int32)

    width = columns // GROUPS
    shards = [w_out] + [
        jnp.concatenate(
            [
                w_qkv[:, :, kind * columns + g * width : kind * columns + (g + 1) * width]
                for kind in range(3)
            ],
            axis=-1,
        )
        for g in range(GROUPS)
    ]
    final = len(shards) - 1
    line_steps = [(w, k, 0) for w in range(final) for k in range(1, lines)]
    line_steps += [(final, k, m) for k in range(1, lines) for m in range(columns_wide)]
    cross_steps = [(w, k, m) for w in range(final) for k in range(lines) for m in range(1, columns_wide)]
    cross_steps += [(final, 0, m) for m in range(1, columns_wide)]

    def rank(step):
        early = 3 if step in cross_steps and step[0] == final else 0
        return 2 * step[0] + 2 * step[1] - early, step[0], step[2]

    line_steps, cross_steps = sorted(line_steps, key=rank), sorted(cross_steps, key=rank)
    held = {(w, 0, 0): shard for w, shard in enumerate(shards)}
    recent, pending = [], []
    while line_steps or cross_steps:
        landed = []
        after = recent[-2] if len(recent) > 1 else []
        ready = [s for s in line_steps if (s[0], s[1] - 1, s[2]) in held]
        if ready:
            step = ready[0]
            line_steps.remove(step)
            operand = held[(step[0], step[1] - 1, step[2])]
            landed.append((step, lax.ppermute(tie(operand, after), "frame", along)))
        ready = [s for s in cross_steps if (s[0], s[1], 0) in held]
        if ready:
            step = ready[0]
            cross_steps.remove(step)
            operand = held[(step[0], step[1], 0)]
            landed.append((step, lax.ppermute(tie(operand, after), "frame", turn(step[2]))))
        recent.append([value for _, value in landed])
        held.update(pending)
        pending = landed
    held.update(pending)
    slots = [
        [held[(w, k, m)] for k in range(lines) for m in range(columns_wide)]
        for w in range(len(shards))
    ]

    wide_in = inputs.astype(F32)
    inverse_rms = lax.rsqrt(jnp.mean(wide_in * wide_in, axis=-1, keepdims=True) + EPSILON)
    normed = (wide_in * inverse_rms * norm_gain).astype(BF16).transpose(1, 0, 2)
    rows = inputs.transpose(1, 0, 2)
    grad_rows = grad_out.transpose(1, 0, 2)

    def exchange(values):
        return lax.all_to_all(values, "cb", split_axis=0, concat_axis=0, tiled=True)

    def joined(values):
        return values.reshape((values.shape[0] * values.shape[1],) + values.shape[2:])

    grad_context = joined(exchange(project(source, grad_rows, slots[0], parts, True)))
    returned, total = [], None
    for g in range(GROUPS):
        weight = slots[1 + g]
        qkv = joined(exchange(project(source, normed, weight, parts, False)))
        mixed = attend(g, HEADS // GROUPS, qkv, grad_context)
        back = exchange(mixed.reshape((parts, codebooks) + mixed.shape[1:]))
        returned.append(back)
        epilogue = (rows, grad_rows, norm_gain) if g == GROUPS - 1 else None
        total = backward(source, back, weight, total, epilogue)
    outputs = output(source, rows, returned, slots[0])
    return outputs.transpose(1, 0, 2), total.transpose(1, 0, 2)


def solution(mesh):
    count = mesh.shape["frame"]
    columns_wide = 2 if count % 2 == 0 else 1
    return jax.shard_map(
        functools.partial(body, count // columns_wide, columns_wide),
        mesh=mesh,
        in_specs=(
            P("frame", "cb", None),
            P(),
            P("cb", "frame", None),
            P("cb", "frame", None),
            P("frame", "cb", None),
        ),
        out_specs=(P("frame", "cb", None), P("frame", "cb", None)),
        check_vma=False,
    )
```

```python
import functools

import jax
import jax.numpy as jnp
from jax import lax
from jax.experimental import pallas as pl
from jax.experimental.pallas import tpu as pltpu
from jax.sharding import PartitionSpec as P

HEADS = 16
GROUP_HEADS = (4, 4, 4, 4)
KERNEL_STEPS = 1
EXCHANGE_STEPS = 2
CROSS_FIRST = 3
CROSS_EARLY = 1.5
ORDER = (0, 1, 2, 3, 4)
VMEM_LIMIT = 60 * 1024 * 1024
EPSILON = 1e-05
F32 = jnp.float32
BF16 = jnp.bfloat16
FRAME_BLOCK = 16
HALF = 8


def params():
    return pltpu.CompilerParams(
        dimension_semantics=("arbitrary",), vmem_limit_bytes=VMEM_LIMIT
    )


def cost(flops, byte_count):
    return pl.CostEstimate(flops=flops, bytes_accessed=byte_count, transcendentals=0)


def fill(layout, source_ref, refs, whole_ref):
    refs = list(refs)
    for way, first, count in layout:
        depth, width = refs[0].shape[1:]
        for slot in range(count):
            start = pl.multiple_of(source_ref[way, slot] * depth, depth)
            whole_ref[pl.ds(start, depth), first : first + width] = refs.pop(0)[0]


def layout_of(pieces):
    layout, slots, first = [], [], 0
    for way, shards in pieces:
        layout.append((way, first, len(shards)))
        slots += shards
        first += shards[0].shape[2]
    depth = sum(shard.shape[1] for shard in pieces[0][1])
    specs = [pl.BlockSpec((1,) + shard.shape[1:], lambda c: (c, 0, 0)) for shard in slots]
    return tuple(layout), slots, specs, (depth, first)


def project_kernel(layout, back, source_ref, rows_ref, *refs):
    out_ref, whole_ref = refs[-2:]
    fill(layout, source_ref, refs[:-2], whole_ref)
    contract = ((1,), (1,)) if back else ((1,), (0,))
    result = lax.dot_general(
        rows_ref[0], whole_ref[...], (contract, ((), ())), preferred_element_type=F32
    )
    out_ref[...] = result.astype(BF16).reshape(out_ref.shape)


def project(source, rows, pieces, parts, back):
    codebooks, frames, columns = rows.shape
    layout, slots, specs, (depth, width) = layout_of(pieces)
    out_columns = depth if back else width
    share = frames // parts
    return pl.pallas_call(
        functools.partial(project_kernel, layout, back),
        grid=(codebooks,),
        in_specs=[
            pl.BlockSpec(memory_space=pltpu.SMEM),
            pl.BlockSpec((1, frames, columns), lambda c: (c, 0, 0)),
        ]
        + specs,
        out_specs=pl.BlockSpec((parts, 1, share, out_columns), lambda c: (0, c, 0, 0)),
        out_shape=jax.ShapeDtypeStruct((parts, codebooks, share, out_columns), BF16),
        scratch_shapes=[pltpu.VMEM((depth, width), BF16)],
        compiler_params=params(),
        cost_estimate=cost(
            2 * codebooks * frames * depth * width, 2 * codebooks * depth * (width + frames)
        ),
        name="project_back" if back else "project",
    )(source, rows, *slots)


def attend_kernel(heads, qkv_ref, grad_ref, *out_refs):
    codebooks, _, width = grad_ref.shape
    head_width = width // heads
    rows = codebooks * HALF
    factor = head_width ** (-0.5)
    row = lax.broadcasted_iota(jnp.int32, (rows, rows), 0)
    column = lax.broadcasted_iota(jnp.int32, (rows, rows), 1)
    allowed = jnp.logical_and(row % HALF == column % HALF, row >= column)[None]
    lane_head = lax.broadcasted_iota(jnp.int32, (rows, width), 1) // head_width

    def wide(ref, first):
        values = ref[:, :, first : first + width].astype(F32)
        return values.reshape(codebooks, FRAME_BLOCK // HALF, HALF, width)

    def stacked(values):
        pieces = [jnp.where(lane_head == h, values, 0.0).astype(BF16) for h in range(heads)]
        return jnp.concatenate(pieces, axis=0)

    def beside(values):
        return jnp.concatenate([values[h * rows : (h + 1) * rows] for h in range(heads)], axis=1)

    def dot(left, right, left_dim, right_dim):
        return lax.dot_general(
            left, right, (((left_dim,), (right_dim,)), ((), ())), preferred_element_type=F32
        )

    parts = [wide(qkv_ref, 0), wide(qkv_ref, width), wide(qkv_ref, 2 * width), wide(grad_ref, 0)]
    results = [[], [], [], []]
    for half in range(FRAME_BLOCK // HALF):
        q, k, v, g = [part[:, half].reshape(rows, width) for part in parts]
        q_heads, k_heads, v_heads, g_heads = stacked(q), stacked(k), stacked(v), stacked(g)
        scores = dot(q_heads, k.astype(BF16), 1, 1).reshape(heads, rows, rows) * factor
        scores = jnp.where(allowed, scores, -jnp.inf)
        weights = jnp.exp(scores - jnp.max(scores, axis=-1, keepdims=True))
        probs = weights / jnp.sum(weights, axis=-1, keepdims=True)
        grad_probs = dot(g_heads, v.astype(BF16), 1, 1).reshape(heads, rows, rows)
        inner = jnp.sum(probs * grad_probs, axis=-1, keepdims=True)
        grad_scores = (probs * (grad_probs - inner) * factor).astype(BF16)
        probs_low = probs.astype(BF16).reshape(heads * rows, rows)
        grad_scores = grad_scores.reshape(heads * rows, rows)
        results[0].append(dot(beside(probs_low), v_heads, 1, 0))
        results[1].append(dot(beside(grad_scores), k_heads, 1, 0))
        results[2].append(dot(grad_scores, q_heads, 0, 0))
        results[3].append(dot(probs_low, g_heads, 0, 0))
    for index, halves in enumerate(results):
        halves = [value.reshape(codebooks, 1, HALF, width) for value in halves]
        whole = jnp.concatenate(halves, axis=1).reshape(codebooks, FRAME_BLOCK, width)
        if len(out_refs) == 2 and index == 0:
            out_refs[0][...] = whole.astype(BF16)
        else:
            start = (index + 1 - len(out_refs)) * width
            out_refs[-1][:, :, start : start + width] = whole.astype(BF16)


def attend(place, heads, split, qkv, grad_context):
    codebooks, frames, columns = qkv.shape
    width = columns // 3
    rows = codebooks * HALF
    counts = (1, 3) if split else (4,)
    return pl.pallas_call(
        functools.partial(attend_kernel, heads),
        grid=(frames // FRAME_BLOCK,),
        in_specs=[
            pl.BlockSpec((codebooks, FRAME_BLOCK, columns), lambda f: (0, f, 0)),
            pl.BlockSpec((codebooks, FRAME_BLOCK, width), lambda f: (0, f, place)),
        ],
        out_specs=[
            pl.BlockSpec((codebooks, FRAME_BLOCK, n * width), lambda f: (0, f, 0)) for n in counts
        ],
        out_shape=[
            jax.ShapeDtypeStruct((codebooks, frames, n * width), BF16) for n in counts
        ],
        compiler_params=params(),
        cost_estimate=cost(
            12 * heads * rows * rows * width * (frames // HALF),
            2 * codebooks * frames * width * 8,
        ),
        name="attend",
    )(qkv, grad_context)


def backward_kernel(layout, first, last, source_ref, back_ref, *refs):
    refs = list(refs)
    whole_ref = refs.pop()
    out_ref = refs.pop()
    total_ref = None if first else refs.pop(0)
    if last:
        rows_ref, grad_ref, gain_ref = refs.pop(0), refs.pop(0), refs.pop(0)
    fill(layout, source_ref, refs, whole_ref)
    frames = out_ref.shape[1]
    width = whole_ref.shape[1]
    grad = back_ref[...].reshape(frames, back_ref.shape[3])[:, -width:]
    total = lax.dot_general(
        grad, whole_ref[...], (((1,), (1,)), ((), ())), preferred_element_type=F32
    )
    if not first:
        total = total + total_ref[0]
    if last:
        rows = rows_ref[0].astype(F32)
        inverse_rms = lax.rsqrt(jnp.mean(rows * rows, axis=-1, keepdims=True) + EPSILON)
        scaled = total * gain_ref[...]
        inner = jnp.mean(scaled * rows, axis=-1, keepdims=True)
        total = grad_ref[0].astype(F32) + inverse_rms * (
            scaled - rows * (inverse_rms * inverse_rms * inner)
        )
    out_ref[0] = total.astype(out_ref.dtype)


def backward(source, returned, pieces, total, epilogue):
    parts, codebooks, share, columns = returned.shape
    frames = parts * share
    layout, slots, slot_specs, (depth, width) = layout_of(pieces)
    row_spec = pl.BlockSpec((1, frames, depth), lambda c: (c, 0, 0))
    operands = [source, returned]
    specs = [
        pl.BlockSpec(memory_space=pltpu.SMEM),
        pl.BlockSpec((parts, 1, share, columns), lambda c: (0, c, 0, 0)),
    ]
    if total is not None:
        operands.append(total)
        specs.append(row_spec)
    if epilogue is not None:
        rows, grad_out, gain = epilogue
        operands += [rows, grad_out, gain.reshape(1, depth)]
        specs += [row_spec, row_spec, pl.BlockSpec((1, depth), lambda c: (0, 0))]
    return pl.pallas_call(
        functools.partial(backward_kernel, layout, total is None, epilogue is not None),
        grid=(codebooks,),
        in_specs=specs + slot_specs,
        out_specs=row_spec,
        out_shape=jax.ShapeDtypeStruct(
            (codebooks, frames, depth), F32 if epilogue is None else BF16
        ),
        scratch_shapes=[pltpu.VMEM((depth, width), BF16)],
        compiler_params=params(),
        cost_estimate=cost(
            2 * codebooks * frames * depth * width, 2 * codebooks * depth * (width + 5 * frames)
        ),
        name="backward",
    )(*operands, *slots)


def output_kernel(layout, groups, source_ref, rows_ref, *refs):
    refs = list(refs)
    whole_ref = refs.pop()
    out_ref = refs.pop()
    fill(layout, source_ref, refs[groups:], whole_ref)
    frames = out_ref.shape[1]
    pieces = [ref[...].reshape(frames, ref.shape[3]) for ref in refs[:groups]]
    result = jnp.dot(
        jnp.concatenate(pieces, axis=1), whole_ref[...], preferred_element_type=F32
    )
    out_ref[0] = (rows_ref[0].astype(F32) + result).astype(BF16)


def output(source, rows, returned, widths, pieces):
    codebooks, frames, columns = rows.shape
    parts, _, share, _ = returned[0].shape
    layout, slots, specs, size = layout_of(pieces)
    row_spec = pl.BlockSpec((1, frames, columns), lambda c: (c, 0, 0))
    return pl.pallas_call(
        functools.partial(output_kernel, layout, len(returned)),
        grid=(codebooks,),
        in_specs=[pl.BlockSpec(memory_space=pltpu.SMEM), row_spec]
        + [pl.BlockSpec((parts, 1, share, wide), lambda c: (0, c, 0, 0)) for wide in widths]
        + specs,
        out_specs=row_spec,
        out_shape=jax.ShapeDtypeStruct(rows.shape, BF16),
        scratch_shapes=[pltpu.VMEM(size, BF16)],
        compiler_params=params(),
        cost_estimate=cost(
            2 * codebooks * frames * columns * columns, 2 * codebooks * columns * (columns + 3 * frames)
        ),
        name="output",
    )(source, rows, *returned, *slots)


def tie(values, after):
    return lax.optimization_barrier((values,) + tuple(after))[0] if after else values


def body(lines, columns_wide, inputs, norm_gain, w_qkv, w_out, grad_out):
    frames, codebooks, columns = inputs.shape
    parts = lax.axis_size("cb")
    count = lines * columns_wide

    place = lax.axis_index("frame")
    line, column = lax.div(place, columns_wide), lax.rem(place, columns_wide)
    along = [(i, (i + columns_wide) % count) for i in range(count)]

    def turn(step):
        return [
            (i, i // columns_wide * columns_wide + (i + step) % columns_wide) for i in range(count)
        ]

    back = jnp.arange(count, dtype=jnp.int32)
    back_line, back_column = back // columns_wide, back % columns_wide
    source = lax.rem(line - back_line + lines, lines) * columns_wide + lax.rem(
        column - back_column + columns_wide, columns_wide
    )
    source = source.astype(jnp.int32)[None]

    head_width = columns // HEADS
    widths = [heads * head_width for heads in GROUP_HEADS]
    starts = [sum(widths[:g]) for g in range(len(widths))]
    final = len(widths) - 1

    def packed(g):
        pieces = [
            w_qkv[:, :, kind * columns + starts[g] : kind * columns + starts[g] + widths[g]]
            for kind in range(3)
        ]
        return jnp.concatenate(pieces, axis=-1)

    shards = [w_out] + [packed(g) for g in range(len(widths))]
    line_steps, cross_steps = [], []
    for w in ORDER:
        first = w == CROSS_FIRST
        for k in range(1, lines):
            line_steps += [(w, k, m) for m in range(columns_wide if first else 1)]
        for m in range(1, columns_wide):
            cross_steps += [(w, k, m) for k in range(1 if first else lines)]
    cross_steps.sort(key=lambda step: ORDER.index(step[0]) - CROSS_EARLY * (step[0] == CROSS_FIRST))
    held = {(w, 0, 0): shard for w, shard in enumerate(shards)}

    wide_in = inputs.astype(F32)
    inverse_rms = lax.rsqrt(jnp.mean(wide_in * wide_in, axis=-1, keepdims=True) + EPSILON)
    normed = (wide_in * inverse_rms * norm_gain).astype(BF16).transpose(1, 0, 2)
    rows = inputs.transpose(1, 0, 2)
    grad_rows = grad_out.transpose(1, 0, 2)
    due = {1: [normed, rows, grad_rows] + shards}
    latest = []

    def join(window, *values):
        due.setdefault(window, []).extend(values)

    def carry():
        after = latest[-1] + due.get(len(latest), []) if latest else []
        landed = []
        for steps, along_line in ((line_steps, True), (cross_steps, False)):
            for step in steps:
                w, k, m = step
                origin = (w, k - 1, m) if along_line else (w, k, 0)
                if origin in held:
                    steps.remove(step)
                    pairs = along if along_line else turn(m)
                    landed.append((step, lax.ppermute(tie(held[origin], after), "frame", pairs)))
                    break
        held.update(landed)
        latest.append([value for _, value in landed])

    def arrived(w):
        return all((w, k, m) in held for k in range(lines) for m in range(columns_wide))

    def weight(w):
        return [(0, [held[(w, k, m)] for k in range(lines) for m in range(columns_wide)])]

    def group(g):
        return weight(1 + g)

    def exchange(values):
        return lax.all_to_all(values, "cb", split_axis=0, concat_axis=0, tiled=True)

    def joined(values):
        return values.reshape((values.shape[0] * values.shape[1],) + values.shape[2:])

    state = {"total": None}
    contexts = []

    def forward(g, step):
        made = project(source, tie(normed, latest[-1]), group(g), parts, False)
        state[g] = joined(exchange(made))
        join(step + KERNEL_STEPS, made)

    def mix(g, step):
        split = g == final
        place, heads = starts[g] // widths[g], GROUP_HEADS[g]
        mixed = attend(place, heads, split, tie(state[g], latest[-1]), state["grad"])
        back = [exchange(m.reshape((parts, codebooks) + m.shape[1:])) for m in mixed]
        join(step + KERNEL_STEPS, *mixed)
        state[g] = back[-1]
        contexts.append(back[0])

    def reverse(g, step):
        epilogue = (rows, grad_rows, norm_gain) if g == final else None
        back = tie(state[g], latest[-1])
        state["total"] = backward(source, back, group(g), state["total"], epilogue)
        join(step + KERNEL_STEPS, state["total"])

    def start(step):
        grad = tie(grad_rows, latest[-1])
        made = project(source, grad, weight(0), parts, True)
        state["grad"] = joined(exchange(made))
        join(step + KERNEL_STEPS, made)
        join(step + EXCHANGE_STEPS, state["grad"])

    waiting, tasks = list(range(len(shards))), []
    while line_steps or cross_steps or waiting or tasks:
        now = len(latest)
        for w in [w for w in waiting if arrived(w)]:
            waiting.remove(w)
            tasks.append((now, 0, start, ()) if w == 0 else (now, w, forward, (w - 1,)))
        ready = sorted(task for task in tasks if task[0] <= now)
        for task in ready[: 1 if line_steps or cross_steps else len(ready)]:
            tasks.remove(task)
            _, _, run, operands = task
            if run is mix and "grad" not in state:
                tasks.append((now + 1,) + task[1:])
                continue
            run(*operands, now)
            if run is forward:
                tasks.append((now + EXCHANGE_STEPS, 10 + operands[0], mix, operands))
            elif run is mix and operands[0] < final:
                tasks.append((now + EXCHANGE_STEPS + 1, 20 + operands[0], reverse, operands))
        carry()
    outputs = output(source, rows, contexts, widths, weight(0))
    reverse(final, len(latest))
    return outputs.transpose(1, 0, 2), state["total"].transpose(1, 0, 2)


def solution(mesh):
    count = mesh.shape["frame"]
    columns_wide = 2 if count % 2 == 0 else 1
    return jax.shard_map(
        functools.partial(body, count // columns_wide, columns_wide),
        mesh=mesh,
        in_specs=(
            P("frame", "cb", None),
            P(),
            P("cb", "frame", None),
            P("cb", "frame", None),
            P("frame", "cb", None),
        ),
        out_specs=(P("frame", "cb", None), P("frame", "cb", None)),
        check_vma=False,
    )
```

```python
import functools

import jax
import jax.numpy as jnp
from jax import lax
from jax.experimental import pallas as pl
from jax.experimental.pallas import tpu as pltpu
from jax.sharding import PartitionSpec as P

HEADS = 16
GROUP_HEADS = (4, 4, 4, 4)
KERNEL_STEPS = 1
EXCHANGE_STEPS = 3
CROSS_FIRST = 4
CROSS_EARLY = 1.5
ORDER = (0, 1, 2, 3, 4)
VMEM_LIMIT = 60 * 1024 * 1024
EPSILON = 1e-05
F32 = jnp.float32
BF16 = jnp.bfloat16
FRAME_BLOCK = 16
HALF = 8


def params():
    return pltpu.CompilerParams(
        dimension_semantics=("arbitrary",), vmem_limit_bytes=VMEM_LIMIT
    )


def cost(flops, byte_count):
    return pl.CostEstimate(flops=flops, bytes_accessed=byte_count, transcendentals=0)


def fill(layout, source_ref, refs, whole_ref):
    refs = list(refs)
    for way, first, count in layout:
        depth, width = refs[0].shape[1:]
        for slot in range(count):
            start = pl.multiple_of(source_ref[way, slot] * depth, depth)
            whole_ref[pl.ds(start, depth), first : first + width] = refs.pop(0)[0]


def layout_of(pieces):
    layout, slots, first = [], [], 0
    for way, shards in pieces:
        layout.append((way, first, len(shards)))
        slots += shards
        first += shards[0].shape[2]
    depth = sum(shard.shape[1] for shard in pieces[0][1])
    specs = [pl.BlockSpec((1,) + shard.shape[1:], lambda c: (c, 0, 0)) for shard in slots]
    return tuple(layout), slots, specs, (depth, first)


def project_kernel(layout, back, source_ref, rows_ref, *refs):
    out_ref, whole_ref = refs[-2:]
    fill(layout, source_ref, refs[:-2], whole_ref)
    contract = ((1,), (1,)) if back else ((1,), (0,))
    result = lax.dot_general(
        rows_ref[0], whole_ref[...], (contract, ((), ())), preferred_element_type=F32
    )
    out_ref[...] = result.astype(BF16).reshape(out_ref.shape)


def project(source, rows, pieces, parts, back):
    codebooks, frames, columns = rows.shape
    layout, slots, specs, (depth, width) = layout_of(pieces)
    out_columns = depth if back else width
    share = frames // parts
    return pl.pallas_call(
        functools.partial(project_kernel, layout, back),
        grid=(codebooks,),
        in_specs=[
            pl.BlockSpec(memory_space=pltpu.SMEM),
            pl.BlockSpec((1, frames, columns), lambda c: (c, 0, 0)),
        ]
        + specs,
        out_specs=pl.BlockSpec((parts, 1, share, out_columns), lambda c: (0, c, 0, 0)),
        out_shape=jax.ShapeDtypeStruct((parts, codebooks, share, out_columns), BF16),
        scratch_shapes=[pltpu.VMEM((depth, width), BF16)],
        compiler_params=params(),
        cost_estimate=cost(
            2 * codebooks * frames * depth * width, 2 * codebooks * depth * (width + frames)
        ),
        name="project_back" if back else "project",
    )(source, rows, *slots)


def attend_kernel(heads, qkv_ref, grad_ref, *out_refs):
    codebooks, _, width = grad_ref.shape
    head_width = width // heads
    rows = codebooks * HALF
    factor = head_width ** (-0.5)
    row = lax.broadcasted_iota(jnp.int32, (rows, rows), 0)
    column = lax.broadcasted_iota(jnp.int32, (rows, rows), 1)
    allowed = jnp.logical_and(row % HALF == column % HALF, row >= column)[None]
    lane_head = lax.broadcasted_iota(jnp.int32, (rows, width), 1) // head_width

    def wide(ref, first):
        values = ref[:, :, first : first + width].astype(F32)
        return values.reshape(codebooks, FRAME_BLOCK // HALF, HALF, width)

    def stacked(values):
        pieces = [jnp.where(lane_head == h, values, 0.0).astype(BF16) for h in range(heads)]
        return jnp.concatenate(pieces, axis=0)

    def beside(values):
        return jnp.concatenate([values[h * rows : (h + 1) * rows] for h in range(heads)], axis=1)

    def dot(left, right, left_dim, right_dim):
        return lax.dot_general(
            left, right, (((left_dim,), (right_dim,)), ((), ())), preferred_element_type=F32
        )

    parts = [wide(qkv_ref, 0), wide(qkv_ref, width), wide(qkv_ref, 2 * width), wide(grad_ref, 0)]
    results = [[], [], [], []]
    for half in range(FRAME_BLOCK // HALF):
        q, k, v, g = [part[:, half].reshape(rows, width) for part in parts]
        q_heads, k_heads, v_heads, g_heads = stacked(q), stacked(k), stacked(v), stacked(g)
        scores = dot(q_heads, k.astype(BF16), 1, 1).reshape(heads, rows, rows) * factor
        scores = jnp.where(allowed, scores, -jnp.inf)
        weights = jnp.exp(scores - jnp.max(scores, axis=-1, keepdims=True))
        probs = weights / jnp.sum(weights, axis=-1, keepdims=True)
        grad_probs = dot(g_heads, v.astype(BF16), 1, 1).reshape(heads, rows, rows)
        inner = jnp.sum(probs * grad_probs, axis=-1, keepdims=True)
        grad_scores = (probs * (grad_probs - inner) * factor).astype(BF16)
        probs_low = probs.astype(BF16).reshape(heads * rows, rows)
        grad_scores = grad_scores.reshape(heads * rows, rows)
        results[0].append(dot(beside(probs_low), v_heads, 1, 0))
        results[1].append(dot(beside(grad_scores), k_heads, 1, 0))
        results[2].append(dot(grad_scores, q_heads, 0, 0))
        results[3].append(dot(probs_low, g_heads, 0, 0))
    for index, halves in enumerate(results):
        halves = [value.reshape(codebooks, 1, HALF, width) for value in halves]
        whole = jnp.concatenate(halves, axis=1).reshape(codebooks, FRAME_BLOCK, width)
        if len(out_refs) == 2 and index == 0:
            out_refs[0][...] = whole.astype(BF16)
        else:
            start = (index + 1 - len(out_refs)) * width
            out_refs[-1][:, :, start : start + width] = whole.astype(BF16)


def attend(place, heads, split, qkv, grad_context):
    codebooks, frames, columns = qkv.shape
    width = columns // 3
    rows = codebooks * HALF
    counts = (1, 3) if split else (4,)
    return pl.pallas_call(
        functools.partial(attend_kernel, heads),
        grid=(frames // FRAME_BLOCK,),
        in_specs=[
            pl.BlockSpec((codebooks, FRAME_BLOCK, columns), lambda f: (0, f, 0)),
            pl.BlockSpec((codebooks, FRAME_BLOCK, width), lambda f: (0, f, place)),
        ],
        out_specs=[
            pl.BlockSpec((codebooks, FRAME_BLOCK, n * width), lambda f: (0, f, 0)) for n in counts
        ],
        out_shape=[
            jax.ShapeDtypeStruct((codebooks, frames, n * width), BF16) for n in counts
        ],
        compiler_params=params(),
        cost_estimate=cost(
            12 * heads * rows * rows * width * (frames // HALF),
            2 * codebooks * frames * width * 8,
        ),
        name="attend",
    )(qkv, grad_context)


def backward_kernel(layout, first, last, source_ref, back_ref, *refs):
    refs = list(refs)
    whole_ref = refs.pop()
    out_ref = refs.pop()
    total_ref = None if first else refs.pop(0)
    if last:
        rows_ref, grad_ref, gain_ref = refs.pop(0), refs.pop(0), refs.pop(0)
    fill(layout, source_ref, refs, whole_ref)
    frames = out_ref.shape[1]
    width = whole_ref.shape[1]
    grad = back_ref[...].reshape(frames, back_ref.shape[3])[:, -width:]
    total = lax.dot_general(
        grad, whole_ref[...], (((1,), (1,)), ((), ())), preferred_element_type=F32
    )
    if not first:
        total = total + total_ref[0]
    if last:
        rows = rows_ref[0].astype(F32)
        inverse_rms = lax.rsqrt(jnp.mean(rows * rows, axis=-1, keepdims=True) + EPSILON)
        scaled = total * gain_ref[...]
        inner = jnp.mean(scaled * rows, axis=-1, keepdims=True)
        total = grad_ref[0].astype(F32) + inverse_rms * (
            scaled - rows * (inverse_rms * inverse_rms * inner)
        )
    out_ref[0] = total.astype(out_ref.dtype)


def backward(source, returned, pieces, total, epilogue):
    parts, codebooks, share, columns = returned.shape
    frames = parts * share
    layout, slots, slot_specs, (depth, width) = layout_of(pieces)
    row_spec = pl.BlockSpec((1, frames, depth), lambda c: (c, 0, 0))
    operands = [source, returned]
    specs = [
        pl.BlockSpec(memory_space=pltpu.SMEM),
        pl.BlockSpec((parts, 1, share, columns), lambda c: (0, c, 0, 0)),
    ]
    if total is not None:
        operands.append(total)
        specs.append(row_spec)
    if epilogue is not None:
        rows, grad_out, gain = epilogue
        operands += [rows, grad_out, gain.reshape(1, depth)]
        specs += [row_spec, row_spec, pl.BlockSpec((1, depth), lambda c: (0, 0))]
    return pl.pallas_call(
        functools.partial(backward_kernel, layout, total is None, epilogue is not None),
        grid=(codebooks,),
        in_specs=specs + slot_specs,
        out_specs=row_spec,
        out_shape=jax.ShapeDtypeStruct(
            (codebooks, frames, depth), F32 if epilogue is None else BF16
        ),
        scratch_shapes=[pltpu.VMEM((depth, width), BF16)],
        compiler_params=params(),
        cost_estimate=cost(
            2 * codebooks * frames * depth * width, 2 * codebooks * depth * (width + 5 * frames)
        ),
        name="backward",
    )(*operands, *slots)


def output_kernel(layout, groups, source_ref, rows_ref, *refs):
    refs = list(refs)
    whole_ref = refs.pop()
    out_ref = refs.pop()
    fill(layout, source_ref, refs[groups:], whole_ref)
    frames = out_ref.shape[1]
    pieces = [ref[...].reshape(frames, ref.shape[3]) for ref in refs[:groups]]
    result = jnp.dot(
        jnp.concatenate(pieces, axis=1), whole_ref[...], preferred_element_type=F32
    )
    out_ref[0] = (rows_ref[0].astype(F32) + result).astype(BF16)


def output(source, rows, returned, widths, pieces):
    codebooks, frames, columns = rows.shape
    parts, _, share, _ = returned[0].shape
    layout, slots, specs, size = layout_of(pieces)
    row_spec = pl.BlockSpec((1, frames, columns), lambda c: (c, 0, 0))
    return pl.pallas_call(
        functools.partial(output_kernel, layout, len(returned)),
        grid=(codebooks,),
        in_specs=[pl.BlockSpec(memory_space=pltpu.SMEM), row_spec]
        + [pl.BlockSpec((parts, 1, share, wide), lambda c: (0, c, 0, 0)) for wide in widths]
        + specs,
        out_specs=row_spec,
        out_shape=jax.ShapeDtypeStruct(rows.shape, BF16),
        scratch_shapes=[pltpu.VMEM(size, BF16)],
        compiler_params=params(),
        cost_estimate=cost(
            2 * codebooks * frames * columns * columns, 2 * codebooks * columns * (columns + 3 * frames)
        ),
        name="output",
    )(source, rows, *returned, *slots)


def tie(values, after):
    return lax.optimization_barrier((values,) + tuple(after))[0] if after else values


def body(lines, columns_wide, inputs, norm_gain, w_qkv, w_out, grad_out):
    frames, codebooks, columns = inputs.shape
    parts = lax.axis_size("cb")
    count = lines * columns_wide

    place = lax.axis_index("frame")
    line, column = lax.div(place, columns_wide), lax.rem(place, columns_wide)
    along = [(i, (i + columns_wide) % count) for i in range(count)]

    def turn(step):
        return [
            (i, i // columns_wide * columns_wide + (i + step) % columns_wide) for i in range(count)
        ]

    back = jnp.arange(count, dtype=jnp.int32)
    back_line, back_column = back // columns_wide, back % columns_wide
    source = lax.rem(line - back_line + lines, lines) * columns_wide + lax.rem(
        column - back_column + columns_wide, columns_wide
    )
    source = source.astype(jnp.int32)[None]

    head_width = columns // HEADS
    widths = [heads * head_width for heads in GROUP_HEADS]
    starts = [sum(widths[:g]) for g in range(len(widths))]
    final = len(widths) - 1

    def packed(g):
        pieces = [
            w_qkv[:, :, kind * columns + starts[g] : kind * columns + starts[g] + widths[g]]
            for kind in range(3)
        ]
        return jnp.concatenate(pieces, axis=-1)

    shards = [w_out] + [packed(g) for g in range(len(widths))]
    line_steps, cross_steps = [], []
    for w in ORDER:
        first = w == CROSS_FIRST
        for k in range(1, lines):
            line_steps += [(w, k, m) for m in range(columns_wide if first else 1)]
        for m in range(1, columns_wide):
            cross_steps += [(w, k, m) for k in range(1 if first else lines)]
    cross_steps.sort(key=lambda step: ORDER.index(step[0]) - CROSS_EARLY * (step[0] == CROSS_FIRST))
    held = {(w, 0, 0): shard for w, shard in enumerate(shards)}

    wide_in = inputs.astype(F32)
    inverse_rms = lax.rsqrt(jnp.mean(wide_in * wide_in, axis=-1, keepdims=True) + EPSILON)
    normed = (wide_in * inverse_rms * norm_gain).astype(BF16).transpose(1, 0, 2)
    rows = inputs.transpose(1, 0, 2)
    grad_rows = grad_out.transpose(1, 0, 2)
    due = {1: [normed, rows, grad_rows] + shards}
    latest = []

    def join(window, *values):
        due.setdefault(window, []).extend(values)

    def carry():
        after = latest[-1] + due.get(len(latest), []) if latest else []
        landed = []
        for steps, along_line in ((line_steps, True), (cross_steps, False)):
            for step in steps:
                w, k, m = step
                origin = (w, k - 1, m) if along_line else (w, k, 0)
                if origin in held:
                    steps.remove(step)
                    pairs = along if along_line else turn(m)
                    landed.append((step, lax.ppermute(tie(held[origin], after), "frame", pairs)))
                    break
        held.update(landed)
        latest.append([value for _, value in landed])

    def arrived(w):
        return all((w, k, m) in held for k in range(lines) for m in range(columns_wide))

    def weight(w):
        return [(0, [held[(w, k, m)] for k in range(lines) for m in range(columns_wide)])]

    def group(g):
        return weight(1 + g)

    sent = []

    def exchange(values):
        values = tie(values, sent[-1:])
        sent.append(lax.all_to_all(values, "cb", split_axis=0, concat_axis=0, tiled=True))
        return sent[-1]

    def joined(values):
        return values.reshape((values.shape[0] * values.shape[1],) + values.shape[2:])

    state = {"total": None}
    contexts = []

    def forward(g, step):
        made = project(source, tie(normed, latest[-1]), group(g), parts, False)
        join(step + KERNEL_STEPS, made)
        if g < final:
            state[g] = joined(exchange(made))
            return
        state[g] = joined(exchange(tie(made, [state[g - 1]])))
        for h in range(final - 1):
            reverse(h, [made])

    def mix(g, step):
        split = g == final
        place, heads = starts[g] // widths[g], GROUP_HEADS[g]
        after = [state["total"]] if split else latest[-1]
        mixed = attend(place, heads, split, tie(state[g], after), state["grad"])
        join(step + KERNEL_STEPS, *mixed)
        mixed = [m.reshape((parts, codebooks) + m.shape[1:]) for m in mixed]
        contexts.append(exchange(mixed[0]))
        if split:
            reverse(g - 1, [mixed[0]])
            state[g] = exchange(tie(mixed[1], [state["total"]]))
        else:
            state[g] = contexts[-1]

    def reverse(g, after):
        epilogue = (rows, grad_rows, norm_gain) if g == final else None
        back = tie(state[g], after)
        state["total"] = backward(source, back, group(g), state["total"], epilogue)

    def start(step):
        grad = tie(grad_rows, latest[-1])
        made = project(source, grad, weight(0), parts, True)
        state["grad"] = joined(exchange(made))
        join(step + KERNEL_STEPS, made)
        join(step + EXCHANGE_STEPS, state["grad"])

    waiting, tasks = list(range(len(shards))), []
    while line_steps or cross_steps or waiting or tasks:
        now = len(latest)
        for w in [w for w in waiting if arrived(w)]:
            waiting.remove(w)
            tasks.append((now, 0, start, ()) if w == 0 else (now, w, forward, (w - 1,)))
        ready = sorted((task for task in tasks if task[0] <= now), key=lambda task: task[:2])
        for task in ready[: 1 if line_steps or cross_steps else len(ready)]:
            tasks.remove(task)
            _, _, run, operands = task
            if run is mix and "grad" not in state:
                tasks.append((now + 1,) + task[1:])
                continue
            run(*operands, now)
            if run is forward:
                tasks.append((now + EXCHANGE_STEPS, 10 + operands[0], mix, operands))
        carry()
    outputs = output(source, rows, contexts, widths, weight(0))
    reverse(final, [])
    return outputs.transpose(1, 0, 2), state["total"].transpose(1, 0, 2)


def solution(mesh):
    count = mesh.shape["frame"]
    columns_wide = 2 if count % 2 == 0 else 1
    return jax.shard_map(
        functools.partial(body, count // columns_wide, columns_wide),
        mesh=mesh,
        in_specs=(
            P("frame", "cb", None),
            P(),
            P("cb", "frame", None),
            P("cb", "frame", None),
            P("frame", "cb", None),
        ),
        out_specs=(P("frame", "cb", None), P("frame", "cb", None)),
        check_vma=False,
    )
```

```python
import functools

import jax
import jax.numpy as jnp
from jax import lax
from jax.experimental import pallas as pl
from jax.experimental.pallas import tpu as pltpu
from jax.sharding import PartitionSpec as P

HEADS = 16
GROUP_HEADS = (4, 4, 4, 4)
KERNEL_STEPS = 1
EXCHANGE_STEPS = 3
CROSS_FIRST = 4
CROSS_EARLY = 1.5
ORDER = (0, 1, 2, 3, 4)
VMEM_LIMIT = 60 * 1024 * 1024
EPSILON = 1e-05
F32 = jnp.float32
BF16 = jnp.bfloat16
FRAME_BLOCK = 16
HALF = 8


def params():
    return pltpu.CompilerParams(
        dimension_semantics=("arbitrary",), vmem_limit_bytes=VMEM_LIMIT
    )


def cost(flops, byte_count):
    return pl.CostEstimate(flops=flops, bytes_accessed=byte_count, transcendentals=0)


def fill(layout, source_ref, refs, whole_ref):
    refs = list(refs)
    for way, first, count in layout:
        depth, width = refs[0].shape[1:]
        for slot in range(count):
            start = pl.multiple_of(source_ref[way, slot] * depth, depth)
            whole_ref[pl.ds(start, depth), first : first + width] = refs.pop(0)[0]


def layout_of(pieces):
    layout, slots, first = [], [], 0
    for way, shards in pieces:
        layout.append((way, first, len(shards)))
        slots += shards
        first += shards[0].shape[2]
    depth = sum(shard.shape[1] for shard in pieces[0][1])
    specs = [pl.BlockSpec((1,) + shard.shape[1:], lambda c: (c, 0, 0)) for shard in slots]
    return tuple(layout), slots, specs, (depth, first)


def project_kernel(layout, back, source_ref, rows_ref, *refs):
    out_ref, whole_ref = refs[-2:]
    fill(layout, source_ref, refs[:-2], whole_ref)
    contract = ((1,), (1,)) if back else ((1,), (0,))
    result = lax.dot_general(
        rows_ref[0], whole_ref[...], (contract, ((), ())), preferred_element_type=F32
    )
    out_ref[...] = result.astype(BF16).reshape(out_ref.shape)


def project(source, rows, pieces, parts, back):
    codebooks, frames, columns = rows.shape
    layout, slots, specs, (depth, width) = layout_of(pieces)
    out_columns = depth if back else width
    share = frames // parts
    return pl.pallas_call(
        functools.partial(project_kernel, layout, back),
        grid=(codebooks,),
        in_specs=[
            pl.BlockSpec(memory_space=pltpu.SMEM),
            pl.BlockSpec((1, frames, columns), lambda c: (c, 0, 0)),
        ]
        + specs,
        out_specs=pl.BlockSpec((parts, 1, share, out_columns), lambda c: (0, c, 0, 0)),
        out_shape=jax.ShapeDtypeStruct((parts, codebooks, share, out_columns), BF16),
        scratch_shapes=[pltpu.VMEM((depth, width), BF16)],
        compiler_params=params(),
        cost_estimate=cost(
            2 * codebooks * frames * depth * width, 2 * codebooks * depth * (width + frames)
        ),
        name="project_back" if back else "project",
    )(source, rows, *slots)


def attend_kernel(heads, qkv_ref, grad_ref, *out_refs):
    codebooks, _, width = grad_ref.shape
    head_width = width // heads
    rows = codebooks * HALF
    factor = head_width ** (-0.5)
    row = lax.broadcasted_iota(jnp.int32, (rows, rows), 0)
    column = lax.broadcasted_iota(jnp.int32, (rows, rows), 1)
    allowed = jnp.logical_and(row % HALF == column % HALF, row >= column)[None]
    lane_head = lax.broadcasted_iota(jnp.int32, (rows, width), 1) // head_width

    def wide(ref, first):
        values = ref[:, :, first : first + width].astype(F32)
        return values.reshape(codebooks, FRAME_BLOCK // HALF, HALF, width)

    def stacked(values):
        pieces = [jnp.where(lane_head == h, values, 0.0).astype(BF16) for h in range(heads)]
        return jnp.concatenate(pieces, axis=0)

    def beside(values):
        return jnp.concatenate([values[h * rows : (h + 1) * rows] for h in range(heads)], axis=1)

    def dot(left, right, left_dim, right_dim):
        return lax.dot_general(
            left, right, (((left_dim,), (right_dim,)), ((), ())), preferred_element_type=F32
        )

    parts = [wide(qkv_ref, 0), wide(qkv_ref, width), wide(qkv_ref, 2 * width), wide(grad_ref, 0)]
    results = [[], [], [], []]
    for half in range(FRAME_BLOCK // HALF):
        q, k, v, g = [part[:, half].reshape(rows, width) for part in parts]
        q_heads, k_heads, v_heads, g_heads = stacked(q), stacked(k), stacked(v), stacked(g)
        scores = dot(q_heads, k.astype(BF16), 1, 1).reshape(heads, rows, rows) * factor
        scores = jnp.where(allowed, scores, -jnp.inf)
        weights = jnp.exp(scores - jnp.max(scores, axis=-1, keepdims=True))
        probs = weights * (1.0 / jnp.sum(weights, axis=-1, keepdims=True))
        grad_probs = dot(g_heads, v.astype(BF16), 1, 1).reshape(heads, rows, rows)
        inner = jnp.sum(probs * grad_probs, axis=-1, keepdims=True)
        grad_scores = (probs * (grad_probs - inner) * factor).astype(BF16)
        probs_low = probs.astype(BF16).reshape(heads * rows, rows)
        grad_scores = grad_scores.reshape(heads * rows, rows)
        results[0].append(dot(beside(probs_low), v_heads, 1, 0))
        results[1].append(dot(beside(grad_scores), k_heads, 1, 0))
        results[2].append(dot(grad_scores, q_heads, 0, 0))
        results[3].append(dot(probs_low, g_heads, 0, 0))
    for index, halves in enumerate(results):
        halves = [value.reshape(codebooks, 1, HALF, width) for value in halves]
        whole = jnp.concatenate(halves, axis=1).reshape(codebooks, FRAME_BLOCK, width)
        if len(out_refs) == 2 and index == 0:
            out_refs[0][...] = whole.astype(BF16)
        else:
            start = (index + 1 - len(out_refs)) * width
            out_refs[-1][:, :, start : start + width] = whole.astype(BF16)


def attend(place, heads, split, qkv, grad_context):
    codebooks, frames, columns = qkv.shape
    width = columns // 3
    rows = codebooks * HALF
    counts = (1, 3) if split else (4,)
    return pl.pallas_call(
        functools.partial(attend_kernel, heads),
        grid=(frames // FRAME_BLOCK,),
        in_specs=[
            pl.BlockSpec((codebooks, FRAME_BLOCK, columns), lambda f: (0, f, 0)),
            pl.BlockSpec((codebooks, FRAME_BLOCK, width), lambda f: (0, f, place)),
        ],
        out_specs=[
            pl.BlockSpec((codebooks, FRAME_BLOCK, n * width), lambda f: (0, f, 0)) for n in counts
        ],
        out_shape=[
            jax.ShapeDtypeStruct((codebooks, frames, n * width), BF16) for n in counts
        ],
        compiler_params=params(),
        cost_estimate=cost(
            12 * heads * rows * rows * width * (frames // HALF),
            2 * codebooks * frames * width * 8,
        ),
        name="attend",
    )(qkv, grad_context)


def backward_kernel(layout, first, last, source_ref, back_ref, *refs):
    refs = list(refs)
    whole_ref = refs.pop()
    out_ref = refs.pop()
    total_ref = None if first else refs.pop(0)
    if last:
        rows_ref, grad_ref, gain_ref = refs.pop(0), refs.pop(0), refs.pop(0)
    fill(layout, source_ref, refs, whole_ref)
    frames = out_ref.shape[1]
    width = whole_ref.shape[1]
    grad = back_ref[...].reshape(frames, back_ref.shape[3])[:, -width:]
    total = lax.dot_general(
        grad, whole_ref[...], (((1,), (1,)), ((), ())), preferred_element_type=F32
    )
    if not first:
        total = total + total_ref[0]
    if last:
        rows = rows_ref[0].astype(F32)
        inverse_rms = lax.rsqrt(jnp.mean(rows * rows, axis=-1, keepdims=True) + EPSILON)
        scaled = total * gain_ref[...]
        inner = jnp.mean(scaled * rows, axis=-1, keepdims=True)
        total = grad_ref[0].astype(F32) + inverse_rms * (
            scaled - rows * (inverse_rms * inverse_rms * inner)
        )
    out_ref[0] = total.astype(out_ref.dtype)


def backward(source, returned, pieces, total, epilogue):
    parts, codebooks, share, columns = returned.shape
    frames = parts * share
    layout, slots, slot_specs, (depth, width) = layout_of(pieces)
    row_spec = pl.BlockSpec((1, frames, depth), lambda c: (c, 0, 0))
    operands = [source, returned]
    specs = [
        pl.BlockSpec(memory_space=pltpu.SMEM),
        pl.BlockSpec((parts, 1, share, columns), lambda c: (0, c, 0, 0)),
    ]
    if total is not None:
        operands.append(total)
        specs.append(row_spec)
    if epilogue is not None:
        rows, grad_out, gain = epilogue
        operands += [rows, grad_out, gain.reshape(1, depth)]
        specs += [row_spec, row_spec, pl.BlockSpec((1, depth), lambda c: (0, 0))]
    return pl.pallas_call(
        functools.partial(backward_kernel, layout, total is None, epilogue is not None),
        grid=(codebooks,),
        in_specs=specs + slot_specs,
        out_specs=row_spec,
        out_shape=jax.ShapeDtypeStruct(
            (codebooks, frames, depth), F32 if epilogue is None else BF16
        ),
        scratch_shapes=[pltpu.VMEM((depth, width), BF16)],
        compiler_params=params(),
        cost_estimate=cost(
            2 * codebooks * frames * depth * width, 2 * codebooks * depth * (width + 5 * frames)
        ),
        name="backward",
    )(*operands, *slots)


def output_kernel(layout, groups, source_ref, rows_ref, *refs):
    refs = list(refs)
    whole_ref = refs.pop()
    out_ref = refs.pop()
    fill(layout, source_ref, refs[groups:], whole_ref)
    frames = out_ref.shape[1]
    pieces = [ref[...].reshape(frames, ref.shape[3]) for ref in refs[:groups]]
    result = jnp.dot(
        jnp.concatenate(pieces, axis=1), whole_ref[...], preferred_element_type=F32
    )
    out_ref[0] = (rows_ref[0].astype(F32) + result).astype(BF16)


def output(source, rows, returned, widths, pieces):
    codebooks, frames, columns = rows.shape
    parts, _, share, _ = returned[0].shape
    layout, slots, specs, size = layout_of(pieces)
    row_spec = pl.BlockSpec((1, frames, columns), lambda c: (c, 0, 0))
    return pl.pallas_call(
        functools.partial(output_kernel, layout, len(returned)),
        grid=(codebooks,),
        in_specs=[pl.BlockSpec(memory_space=pltpu.SMEM), row_spec]
        + [pl.BlockSpec((parts, 1, share, wide), lambda c: (0, c, 0, 0)) for wide in widths]
        + specs,
        out_specs=row_spec,
        out_shape=jax.ShapeDtypeStruct(rows.shape, BF16),
        scratch_shapes=[pltpu.VMEM(size, BF16)],
        compiler_params=params(),
        cost_estimate=cost(
            2 * codebooks * frames * columns * columns, 2 * codebooks * columns * (columns + 3 * frames)
        ),
        name="output",
    )(source, rows, *returned, *slots)


def tie(values, after):
    return lax.optimization_barrier((values,) + tuple(after))[0] if after else values


def body(lines, columns_wide, inputs, norm_gain, w_qkv, w_out, grad_out):
    frames, codebooks, columns = inputs.shape
    parts = lax.axis_size("cb")
    count = lines * columns_wide

    place = lax.axis_index("frame")
    line, column = lax.div(place, columns_wide), lax.rem(place, columns_wide)
    along = [(i, (i + columns_wide) % count) for i in range(count)]

    def turn(step):
        return [
            (i, i // columns_wide * columns_wide + (i + step) % columns_wide) for i in range(count)
        ]

    back = jnp.arange(count, dtype=jnp.int32)
    back_line, back_column = back // columns_wide, back % columns_wide
    source = lax.rem(line - back_line + lines, lines) * columns_wide + lax.rem(
        column - back_column + columns_wide, columns_wide
    )
    source = source.astype(jnp.int32)[None]

    head_width = columns // HEADS
    widths = [heads * head_width for heads in GROUP_HEADS]
    starts = [sum(widths[:g]) for g in range(len(widths))]
    final = len(widths) - 1

    def packed(g):
        pieces = [
            w_qkv[:, :, kind * columns + starts[g] : kind * columns + starts[g] + widths[g]]
            for kind in range(3)
        ]
        return jnp.concatenate(pieces, axis=-1)

    shards = [w_out] + [packed(g) for g in range(len(widths))]
    line_steps, cross_steps = [], []
    for w in ORDER:
        first = w == CROSS_FIRST
        for k in range(1, lines):
            line_steps += [(w, k, m) for m in range(columns_wide if first else 1)]
        for m in range(1, columns_wide):
            cross_steps += [(w, k, m) for k in range(1 if first else lines)]
    cross_steps.sort(key=lambda step: ORDER.index(step[0]) - CROSS_EARLY * (step[0] == CROSS_FIRST))
    held = {(w, 0, 0): shard for w, shard in enumerate(shards)}

    wide_in = inputs.astype(F32)
    inverse_rms = lax.rsqrt(jnp.mean(wide_in * wide_in, axis=-1, keepdims=True) + EPSILON)
    normed = (wide_in * inverse_rms * norm_gain).astype(BF16).transpose(1, 0, 2)
    rows = inputs.transpose(1, 0, 2)
    grad_rows = grad_out.transpose(1, 0, 2)
    due = {1: [normed, rows, grad_rows] + shards}
    latest = []

    def join(window, *values):
        due.setdefault(window, []).extend(values)

    def carry():
        after = latest[-1] + due.get(len(latest), []) if latest else []
        landed = []
        for steps, along_line in ((line_steps, True), (cross_steps, False)):
            for step in steps:
                w, k, m = step
                origin = (w, k - 1, m) if along_line else (w, k, 0)
                if origin in held:
                    steps.remove(step)
                    pairs = along if along_line else turn(m)
                    landed.append((step, lax.ppermute(tie(held[origin], after), "frame", pairs)))
                    break
        held.update(landed)
        latest.append([value for _, value in landed])

    def arrived(w):
        return all((w, k, m) in held for k in range(lines) for m in range(columns_wide))

    def weight(w):
        return [(0, [held[(w, k, m)] for k in range(lines) for m in range(columns_wide)])]

    def group(g):
        return weight(1 + g)

    sent = []

    def exchange(values):
        values = tie(values, sent[-1:])
        sent.append(lax.all_to_all(values, "cb", split_axis=0, concat_axis=0, tiled=True))
        return sent[-1]

    def joined(values):
        return values.reshape((values.shape[0] * values.shape[1],) + values.shape[2:])

    state = {"total": None}
    contexts = []

    def forward(g, step):
        made = project(source, tie(normed, latest[-1]), group(g), parts, False)
        join(step + KERNEL_STEPS, made)
        if g < final:
            state[g] = joined(exchange(made))
            return
        state[g] = joined(exchange(tie(made, [state[g - 1]])))
        for h in range(final - 1):
            reverse(h, [made])

    def mix(g, step):
        split = g == final
        place, heads = starts[g] // widths[g], GROUP_HEADS[g]
        after = [state["total"]] if split else latest[-1]
        mixed = attend(place, heads, split, tie(state[g], after), state["grad"])
        join(step + KERNEL_STEPS, *mixed)
        mixed = [m.reshape((parts, codebooks) + m.shape[1:]) for m in mixed]
        contexts.append(exchange(mixed[0]))
        if split:
            reverse(g - 1, [mixed[0]])
            state[g] = exchange(tie(mixed[1], [state["total"]]))
        else:
            state[g] = contexts[-1]

    def reverse(g, after):
        epilogue = (rows, grad_rows, norm_gain) if g == final else None
        back = tie(state[g], after)
        state["total"] = backward(source, back, group(g), state["total"], epilogue)

    def start(step):
        grad = tie(grad_rows, latest[-1])
        made = project(source, grad, weight(0), parts, True)
        state["grad"] = joined(exchange(made))
        join(step + KERNEL_STEPS, made)
        join(step + EXCHANGE_STEPS, state["grad"])

    waiting, tasks = list(range(len(shards))), []
    while line_steps or cross_steps or waiting or tasks:
        now = len(latest)
        for w in [w for w in waiting if arrived(w)]:
            waiting.remove(w)
            tasks.append((now, 0, start, ()) if w == 0 else (now, w, forward, (w - 1,)))
        ready = sorted((task for task in tasks if task[0] <= now), key=lambda task: task[:2])
        for task in ready[: 1 if line_steps or cross_steps else len(ready)]:
            tasks.remove(task)
            _, _, run, operands = task
            if run is mix and "grad" not in state:
                tasks.append((now + 1,) + task[1:])
                continue
            run(*operands, now)
            if run is forward:
                tasks.append((now + EXCHANGE_STEPS, 10 + operands[0], mix, operands))
        carry()
    outputs = output(source, rows, contexts, widths, weight(0))
    reverse(final, [])
    return outputs.transpose(1, 0, 2), state["total"].transpose(1, 0, 2)


def solution(mesh):
    count = mesh.shape["frame"]
    columns_wide = 2 if count % 2 == 0 else 1
    return jax.shard_map(
        functools.partial(body, count // columns_wide, columns_wide),
        mesh=mesh,
        in_specs=(
            P("frame", "cb", None),
            P(),
            P("cb", "frame", None),
            P("cb", "frame", None),
            P("frame", "cb", None),
        ),
        out_specs=(P("frame", "cb", None), P("frame", "cb", None)),
        check_vma=False,
    )
```
